32 devices in a mesh: dp: 2 (over y), ctx: 4 (over z), tp: 4 (over x, core).
Axes of the slice: x: 2, y: 2, z: 4, core: 2. Of those that a mesh axis runs over, the one named last changes fastest.
Arguments:
- tokens: bfloat16 [1024, 4096], P(('dp', 'ctx'), 'tp'), parts along dimension 0, may hold values from -6 to 6
- expert_ids: int32 [1024, 8], P(('dp', 'ctx')), parts along dimension 0, may hold values from 0 to 127, all different within a row; in each aligned block of 128 rows (0 to 127, 128 to 255, ...) at most 16 rows name the same one
- route_weight: float32 [1024, 8], P(('dp', 'ctx')), parts along dimension 0, may hold values from 0.1 to 1
- gate_weight: bfloat16 [16, 384, 4096], P(('ctx', 'tp')), may hold values from -0.09375 to 0.09375
- up_weight: bfloat16 [16, 384, 4096], P(('ctx', 'tp')), may hold values from -0.09375 to 0.09375
- down_weight: bfloat16 [16, 384, 4096], P(('ctx', 'tp')), may hold values from -0.15625 to 0.15625
Outputs:
- mixed_out: bfloat16 [1024, 4096], P(('dp', 'ctx'), 'tp'), parts along dimension 0
The draws below stay inside these ranges and needn't reach their ends.
There are 2 independent parts, one for each index of `dp`. The reference program is written for one: setup_inputs(seed, part) draws one part's arguments, and reference() takes and returns one part's arrays. A program takes and returns all parts, laid end to end along the dimension named above; an argument that names none is the same for every part. Nothing has to cross between parts.
Inputs may be any that keep to these rules, and one draw needn't show every extreme that they name: `expert_ids`: each token names 8 different experts. In each aligned block of 128 tokens no expert is named by more than 16 tokens, a bound that some block reaches.
All inputs are finite; a program needn't handle non-finite values.
Results may differ from the reference program's by a relative error of at most 0.018.
Values may be sent and summed in bfloat16 or wider, within the bound.
No kernel may reach another device: no remote copies, remote signals or barrier semaphores. Data moves between devices by JAX's collectives and lax.ppermute only.
A program may use at most 128 MiB of HBM per device.

```python
import math
import jax
import jax.numpy as jnp
import numpy as np
from jax import lax

D = 4096
FF = 1536
EXPERTS = 128
TOP = 8
SPLIT = 4
TOK_CTX = 128
EXP_WIN = 4
CAP = 16
TOKENS = 512
N_CTX = 4


def steps_of(rng, shape, cuts, low, high):
    loudness = 1.0
    for dim, parts in cuts:
        steps = jax.random.uniform(jax.random.fold_in(jax.random.fold_in(rng, 6), dim), (parts,), jnp.float32, low / len(cuts), high / len(cuts))
        loudness = loudness * jnp.repeat(jnp.exp(steps), shape[dim] // parts).reshape((-1,) + (1,) * (len(shape) - 1 - dim))
    return loudness


def routed_block(own_key, own, number, rows, number_of, top, bound, skew):
    sequence = jax.random.permutation(own_key, number_of)
    crowded, usual = portions_of(number_of, rows * top, bound, skew, True), portions_of(number_of, rows * top, bound, skew, False)
    places = jnp.arange(number_of)

    def named(sizes, rotation):
        used = int((sizes > 0).sum())
        fixed = max(1, used // 4)
        passed = fixed + (places - fixed + rotation * (used - fixed)) % max(1, number_of - fixed)
        return jnp.zeros((number_of,), jnp.int32).at[sequence[jnp.where(places < fixed, places, passed)]].set(jnp.asarray(sizes, jnp.int32))

    sizes = jnp.where(number % 4 == 0, named(crowded, number // 4), named(usual, number - number // 4 - 1))
    mixed = jax.random.permutation(jax.random.fold_in(own, 3), number_of)
    giver, sink = mixed[0:number_of // 2 * 2:2], mixed[1:number_of // 2 * 2:2]
    room = jnp.minimum(sizes[giver] - 1, bound - sizes[sink]) // 2
    room = jnp.where((giver == sequence[0]) | (sink == sequence[0]) | (sizes[sink] == 0), 0, jnp.maximum(room, 0))
    passed = jax.random.randint(jax.random.fold_in(own, 4), (number_of // 2,), 0, 1 << 20) % (room + 1)
    sizes = sizes.at[giver].add(-passed).at[sink].add(passed)
    labels = jnp.searchsorted(jnp.cumsum(sizes), jnp.arange(rows * top), side="right").astype(jnp.int32)
    table = labels.reshape(top, rows).T
    table = table[jax.random.permutation(jax.random.fold_in(own, 1), rows)]
    rotation = jax.random.randint(jax.random.fold_in(own, 2), (rows, 1), 0, top)
    return jnp.take_along_axis(table, (jnp.arange(top)[None, :] + rotation) % top, axis=1)


def portions_of(amount, total, reach, skew, full):
    loads = [(1 << 20) // math.isqrt(standing ** skew) + 1 for standing in range(1, amount + 1)]
    largest = reach if full else min(reach, max(-(-total // amount), total * loads[0] // sum(loads)))
    least = 1 if total - largest >= amount - 1 else 0
    given, surplus = [largest] + [least] * (amount - 1), total - largest - least * (amount - 1)
    while surplus > 0:
        candidates = [i for i in range(1, amount) if given[i] < largest] or [i for i in range(1, amount) if given[i] < reach]
        whole, left = sum([loads[i] for i in candidates]), surplus
        for i in candidates:
            extra = min(reach - given[i], max(1, left * loads[i] // whole), surplus)
            given[i] = given[i] + extra
            surplus = surplus - extra
    return np.array(given)


def normal_values(rng, shape, deviation, limit, split=(), kind=jnp.bfloat16):
    array = deviation * jax.random.normal(rng, shape, jnp.float32)
    if split:
        array = array * steps_of(rng, shape, split, -0.22, 0.18)
    return jnp.clip(array, -limit, limit).astype(kind)


def setup_inputs(seed: int = 0, part: int = 0) -> dict:
    streams_of = jax.random.split(jax.random.key(seed), 7)
    part_splits = jax.random.split(jax.random.fold_in(streams_of[6], part), 7)
    tokens = normal_values(part_splits[0], (TOKENS, D), 1.0, 6.0, ((0, 4), (1, 4)))
    expert_ids_keys = jax.random.split(jax.random.fold_in(part_splits[1], 1), TOKENS // TOK_CTX)
    expert_ids_turns = jax.random.permutation(jax.random.fold_in(part_splits[1], 3), TOKENS // TOK_CTX)
    expert_ids = jax.vmap(lambda own, number: routed_block(jax.random.fold_in(part_splits[1], 2), own, number, TOK_CTX, EXPERTS, TOP, CAP, 2))(expert_ids_keys, expert_ids_turns).reshape((TOKENS, TOP))
    route_weight = jnp.clip(jnp.exp(math.log(1.0) - 2.3025851 * jax.random.uniform(part_splits[2], (TOKENS, TOP), jnp.float32) ** steps_of(part_splits[2], (TOKENS, TOP), ((0, 4),), -0.2, 0.2)), 0.1, 1.0)
    gate_weight = normal_values(streams_of[3], (EXP_WIN * SPLIT, FF // SPLIT, D), D ** -0.5, 0.09375, ((0, 16),))
    up_weight = normal_values(streams_of[4], (EXP_WIN * SPLIT, FF // SPLIT, D), D ** -0.5, 0.09375, ((0, 16),))
    down_weight = normal_values(streams_of[5], (EXP_WIN * SPLIT, FF // SPLIT, D), FF ** -0.5, 0.15625, ((0, 16),))
    return {"tokens": tokens, "expert_ids": expert_ids, "route_weight": route_weight, "gate_weight": gate_weight, "up_weight": up_weight, "down_weight": down_weight}


def plan(block_ids):
    flat_ids = block_ids.reshape(-1)
    live_route = flat_ids < EXP_WIN
    expert_marks = (flat_ids[:, None] == jnp.arange(EXP_WIN, dtype=jnp.int32)[None, :]).astype(jnp.int32)
    running = jnp.cumsum(expert_marks, axis=0, dtype=jnp.int32) - 1
    slot_index = jnp.sum(running * expert_marks, axis=1, dtype=jnp.int32)
    target_row = jnp.where(live_route, flat_ids * CAP + slot_index, -1).astype(jnp.int32)
    place_index = jnp.arange(EXP_WIN * CAP, dtype=jnp.int32)
    select_mask = (target_row[None, :] == place_index[:, None]).astype(jnp.float32)
    return select_mask.reshape(EXP_WIN * CAP, TOK_CTX, TOP)


def expert_pass(pieces):
    rows, gate_w, up_w, down_w = pieces
    gate_vals = jnp.dot(rows, gate_w.T, preferred_element_type=jnp.float32)
    up_vals = jnp.dot(rows, up_w.T, preferred_element_type=jnp.float32)
    hidden = (jax.nn.silu(gate_vals) * up_vals).astype(jnp.bfloat16)
    quarters = hidden.reshape(rows.shape[0], SPLIT, FF // SPLIT).astype(jnp.float32)
    down_parts = down_w.reshape(SPLIT, FF // SPLIT, D).astype(jnp.float32)
    part_out = jnp.einsum("rqf,qfd->qrd", quarters, down_parts,
                          precision=lax.Precision.HIGHEST).astype(jnp.bfloat16)
    return jnp.sum(part_out.astype(jnp.float32), axis=0)


def reference(tokens, expert_ids, route_weight, gate_weight, up_weight, down_weight):
    gate_full = gate_weight.reshape(EXP_WIN, FF, D)
    up_full = up_weight.reshape(EXP_WIN, FF, D)
    down_full = down_weight.reshape(EXP_WIN, FF, D)
    block_tokens = tokens.reshape(N_CTX, TOK_CTX, D)
    block_ids = expert_ids.reshape(N_CTX, TOK_CTX, TOP)
    block_weight = route_weight.reshape(N_CTX, TOK_CTX, TOP)
    masks = jax.vmap(plan)(block_ids)
    pick_matrix = jnp.sum(masks, axis=3)
    outgoing = jnp.einsum("bpt,btd->bpd", pick_matrix, block_tokens.astype(jnp.float32),
                          precision=lax.Precision.HIGHEST).astype(jnp.bfloat16)
    arranged = outgoing.reshape(N_CTX, EXP_WIN, CAP, D).transpose(1, 0, 2, 3).reshape(EXP_WIN, N_CTX * CAP, D)
    expert_sum = lax.map(expert_pass, (arranged, gate_full, up_full, down_full))
    expert_sum = expert_sum.reshape(EXP_WIN, N_CTX, CAP, D).transpose(1, 0, 2, 3).reshape(N_CTX, EXP_WIN * CAP, D)
    combine = jnp.sum(masks * block_weight[:, None, :, :], axis=3)
    mixed_out = jnp.einsum("bpt,bpd->btd", combine, expert_sum,
                           precision=lax.Precision.HIGHEST)
    return mixed_out.astype(jnp.bfloat16).reshape(TOKENS, D)
```

```python
import functools

import jax
import jax.numpy as jnp
from jax import lax
from jax.experimental import pallas as pl
from jax.experimental.pallas import tpu as pltpu
from jax.sharding import PartitionSpec as P

SPLIT = 4
CAP = 16
CORES = 2
F32 = jnp.float32
BF16 = jnp.bfloat16
VMEM = pl.BlockSpec(memory_space=pltpu.VMEM)
HBM = pl.BlockSpec(memory_space=pltpu.HBM)
NT = (((1,), (1,)), ((), ()))


def swaps(size, mask):
    return [(i, i ^ mask) for i in range(size)]


def turns(size):
    half = size // 2
    return [*range(size - 1, half, -1), *range(1, half), 0, half]


def sds(shape, dtype=BF16):
    return jax.ShapeDtypeStruct(shape, dtype)


def local(kernel, name, out_shape, args, unread=(), cost=0):
    specs = [pl.BlockSpec(memory_space=pl.ANY) if i in unread else VMEM for i in range(len(args))]
    moved = cost or sum(a.size * a.dtype.itemsize for a in args)
    return pl.pallas_call(
        kernel,
        out_shape=out_shape,
        in_specs=specs,
        out_specs=jax.tree.map(lambda _: VMEM, out_shape),
        compiler_params=pltpu.CompilerParams(vmem_limit_bytes=4 * 1024 * 1024),
        cost_estimate=pl.CostEstimate(flops=0, bytes_accessed=moved, transcendentals=0),
        name=name,
    )(*args)


def columns(mask, features):
    at = lax.axis_index("tp") ^ mask
    return pl.ds(pl.multiple_of(at * features, features), features)


def route_kernel(ctx_size, groups, ids_hbm, weight_hbm, tokens_hbm, combine_ref, *refs):
    *row_refs, ids_ref, weight_ref, tokens_ref, sems = refs
    copies = [
        pltpu.make_async_copy(source, target, sems.at[i])
        for i, (source, target) in enumerate(
            ((ids_hbm, ids_ref), (weight_hbm, weight_ref), (tokens_hbm, tokens_ref))
        )
    ]
    for copy in copies:
        copy.start()
    slots = groups * CAP
    top, tok_rows = ids_ref.shape
    places = ctx_size * slots
    here = lax.axis_index("ctx")
    place = lax.broadcasted_iota(jnp.int32, (places, tok_rows), 0)
    order = place // slots
    turn = jnp.zeros_like(place)
    for i, mask in enumerate(turns(ctx_size)):
        turn = jnp.where(order == i, mask, turn)
    expert = (turn ^ here) * groups + (place % slots) // CAP
    slot = (place % CAP).astype(F32)
    before = (
        lax.broadcasted_iota(jnp.int32, (tok_rows, tok_rows), 0)
        < lax.broadcasted_iota(jnp.int32, (tok_rows, tok_rows), 1)
    ).astype(BF16)
    member = jnp.zeros((places, tok_rows), F32)
    weight = jnp.zeros((places, tok_rows), F32)
    copies[0].wait()
    copies[1].wait()
    for k in range(top):
        hit = ids_ref[k : k + 1, :] == expert
        member = jnp.where(hit, 1.0, member)
        weight = jnp.where(hit, weight_ref[k : k + 1, :], weight)
    running = jnp.dot(member.astype(BF16), before, preferred_element_type=F32)
    picked = jnp.where(running == slot, member, 0.0)
    combine_ref[...] = picked * weight
    copies[2].wait()
    rows = jnp.dot(picked.astype(BF16), tokens_ref[...], preferred_element_type=F32).astype(BF16)
    for s, ref in enumerate(row_refs):
        ref[...] = rows[s * slots : (s + 1) * slots]


def route(ids_t, weight_t, tokens, ctx_size, groups):
    tok_rows, features = tokens.shape
    slots = groups * CAP
    args = (ids_t, weight_t, tokens)
    return pl.pallas_call(
        functools.partial(route_kernel, ctx_size, groups),
        out_shape=[sds((ctx_size * slots, tok_rows), F32)] + [sds((slots, features))] * ctx_size,
        in_specs=[HBM] * 3,
        out_specs=[VMEM] * (ctx_size + 1),
        scratch_shapes=[pltpu.VMEM(a.shape, a.dtype) for a in args]
        + [pltpu.SemaphoreType.DMA((3,))],
        compiler_params=pltpu.CompilerParams(vmem_limit_bytes=4 * 1024 * 1024),
        name="route",
    )(*[pltpu.with_memory_space_constraint(a, pltpu.HBM) for a in args])


def load_gate_kernel(cuts, gate_hbm, combine_ref, gate_ref, mix_ref, sems):
    step = gate_ref.shape[0] // cuts
    copies = []
    for c in range(cuts):
        part = pl.ds(c * step, step)
        copies.append(pltpu.make_async_copy(gate_hbm.at[0, part], gate_ref.at[part], sems.at[c]))
    for copy in copies:
        copy.start()
    weight = combine_ref[...].T
    high = weight.astype(BF16)
    mix_ref[...] = jnp.concatenate([high, (weight - high.astype(F32)).astype(BF16)], axis=1)
    for copy in copies:
        copy.wait()


def load_gate(gate_weight, weights, cuts=4):
    places, tok_rows = weights.shape
    return pl.pallas_call(
        functools.partial(load_gate_kernel, cuts),
        out_shape=[sds(gate_weight.shape[1:]), sds((tok_rows, 2 * places))],
        in_specs=[HBM, VMEM],
        out_specs=[VMEM] * 2,
        scratch_shapes=[pltpu.SemaphoreType.DMA((cuts,))],
        compiler_params=pltpu.CompilerParams(vmem_limit_bytes=8 * 1024 * 1024),
        cost_estimate=pl.CostEstimate(
            flops=0, bytes_accessed=4 * gate_weight.size, transcendentals=0
        ),
        name="load_gate",
    )(pltpu.with_memory_space_constraint(gate_weight, pltpu.HBM), weights)


def mark_kernel(_, out_ref):
    out_ref[...] = jnp.zeros(out_ref.shape, F32)


def load_up_kernel(x_ref, gate_ref, up_hbm, up_ref, gate_out, up_out, sems):
    features = x_ref.shape[1]
    copies = []
    for mask in range(up_ref.shape[1] // features):
        part = columns(mask, features)
        copies.append(
            pltpu.make_async_copy(up_hbm.at[0, :, part], up_ref.at[:, part], sems.at[mask])
        )
    for copy in copies:
        copy.start()
    x = x_ref[...]
    own = columns(0, features)
    gate_out[...] = lax.dot_general(gate_ref[:, own], x, NT, preferred_element_type=F32)
    copies[0].wait()
    up_out[...] = lax.dot_general(up_ref[:, own], x, NT, preferred_element_type=F32)
    for copy in copies[1:]:
        copy.wait()


def load_up(x, gate, up_weight):
    rows, features = x.shape
    units, width = gate.shape
    return pl.pallas_call(
        load_up_kernel,
        out_shape=[sds((units, width))] + [sds((units, rows), F32)] * 2,
        in_specs=[VMEM, VMEM, HBM],
        out_specs=[VMEM] * 3,
        scratch_shapes=[pltpu.SemaphoreType.DMA((width // features,))],
        compiler_params=pltpu.CompilerParams(vmem_limit_bytes=8 * 1024 * 1024),
        cost_estimate=pl.CostEstimate(
            flops=0, bytes_accessed=4 * up_weight.size, transcendentals=0
        ),
        name="load_up",
    )(x, gate, pltpu.with_memory_space_constraint(up_weight, pltpu.HBM))


def stack_kernel(places, *refs):
    out_ref = refs[-1]
    for place, ref in zip(places, refs[-1 - len(places) : -1]):
        out_ref[place * ref.shape[0] : (place + 1) * ref.shape[0], :] = ref[...]


def stack(pieces, name, after, places=None):
    places = places or list(range(len(pieces)))
    rows = len(pieces) * pieces[0].shape[0]
    return local(
        functools.partial(stack_kernel, places),
        name,
        sds((rows, pieces[0].shape[1])),
        (*after, *pieces),
        unread=range(len(after)),
    )


def grow(chunks, masks, gate_ref, up_ref, sums):
    gate_vals, up_vals = sums
    for ref, mask in zip(chunks, masks):
        own = columns(mask, ref.shape[1])
        x = ref[...]
        gate_part = lax.dot_general(gate_ref[:, own], x, NT, preferred_element_type=F32)
        up_part = lax.dot_general(up_ref[:, own], x, NT, preferred_element_type=F32)
        gate_vals = gate_vals + gate_part
        up_vals = up_vals + up_part
    return gate_vals, up_vals


def grow_kernel(masks, *refs):
    chunks, (gate_ref, up_ref, gate_in, up_in, gate_out, up_out) = refs[:-6], refs[-6:]
    sums = (gate_in[...], up_in[...])
    gate_out[...], up_out[...] = grow(chunks, masks, gate_ref, up_ref, sums)


def expert_kernel(masks, out_masks, *refs):
    chunks = refs[: len(masks)]
    gate_ref, up_ref, down_ref, gate_in, up_in, hidden_ref, out_ref = refs[len(masks) :]
    sums = (gate_in[...], up_in[...])
    gate_vals, up_vals = grow(chunks, masks, gate_ref, up_ref, sums)
    hidden = (gate_vals / (1.0 + jnp.exp(-gate_vals)) * up_vals).T.astype(BF16)
    hidden_ref[...] = hidden
    shrink(hidden, out_masks, down_ref, out_ref)


def shrink(hidden, masks, down_ref, out_ref):
    rows, features = hidden.shape[0], out_ref.shape[1]
    for i, mask in enumerate(masks):
        down = down_ref[:, columns(mask, features)]
        out = jnp.dot(hidden, down, preferred_element_type=F32)
        out_ref[i * rows : (i + 1) * rows, :] = out.astype(BF16)


def shrink_kernel(masks, hidden_ref, down_ref, *refs):
    out_ref = refs[-1]
    shrink(hidden_ref[...], masks, down_ref, out_ref)


def pair_kernel(rows, own_ref, other_ref, *out_refs):
    count = out_refs[0].shape[0]
    for j, ref in enumerate(out_refs):
        at = slice(j * rows, j * rows + count)
        ref[...] = (own_ref[at, :].astype(F32) + other_ref[at, :].astype(F32)).astype(BF16)


def tail_kernel(own_ref, other_ref, own_away_ref, other_away_ref, out_ref):
    rows = own_ref.shape[0]
    for j in range(out_ref.shape[0] // CAP):
        mine, others = (own_ref, other_ref) if j == 0 else (own_away_ref, other_away_ref)
        at = slice(max(j, 1) * rows - CAP, max(j, 1) * rows)
        total = mine[at, :].astype(F32) + others[at, :].astype(F32)
        out_ref[j * CAP : (j + 1) * CAP, :] = total.astype(BF16)


def split_kernel(in_ref, *out_refs):
    for j, ref in enumerate(out_refs):
        ref[...] = in_ref[j * CAP : (j + 1) * CAP, :]


def group_sums(groups, parts):
    chips = len(parts)
    chip = lax.axis_index("tp") // CORES
    per_group = chips // groups
    totals = []
    for g in range(groups):
        total = None
        for j, term in enumerate(parts):
            if groups > 1:
                term = jnp.where((chip ^ j) // per_group == g, term, 0.0)
            total = term if total is None else total + term
        totals.append(total.astype(BF16))
    return totals


def total_kernel(groups, chips, own_ref, other_ref, *refs):
    part_refs, out_refs = refs[: chips - 1], refs[chips - 1 :]
    count = part_refs[0].shape[0]
    parts = [own_ref[:count, :].astype(F32) + other_ref[:count, :].astype(F32)]
    parts += [ref[...].astype(F32) for ref in part_refs]
    for g, total in enumerate(group_sums(groups, parts)):
        for s, ref in enumerate(out_refs):
            ref[g * CAP : (g + 1) * CAP, :] = total[s * CAP : (s + 1) * CAP]


def combine_kernel(order, groups, cuts, mix_ref, *refs):
    out_hbm, out_ref, sems = refs[-3:]
    count = len(order)
    back_refs, part_refs = refs[:count], refs[count:-3]
    back_refs = [back_refs[i] for i in order]
    mix = mix_ref[...]
    step = out_ref.shape[1] // cuts
    copies = []
    for c in range(cuts):
        part = slice(c * step, (c + 1) * step)
        parts = [ref[:, part].astype(F32) for ref in part_refs]
        back = [ref[:, part] for ref in back_refs] + group_sums(groups, parts)
        back = jnp.concatenate(back * 2, axis=0)
        out_ref[:, part] = jnp.dot(mix, back, preferred_element_type=F32).astype(BF16)
        copies.append(
            pltpu.make_async_copy(out_ref.at[:, part], out_hbm.at[:, part], sems.at[c])
        )
        copies[c].start()
    for copy in copies:
        copy.wait()


def combine(mix, order, groups, backs, parts, cuts=2):
    shape = sds((mix.shape[0], backs[0].shape[1]))
    args = (mix, *backs, *parts)
    return pl.pallas_call(
        functools.partial(combine_kernel, order, groups, cuts),
        out_shape=shape,
        in_specs=[VMEM] * len(args),
        out_specs=HBM,
        scratch_shapes=[pltpu.VMEM(shape.shape, BF16), pltpu.SemaphoreType.DMA((cuts,))],
        compiler_params=pltpu.CompilerParams(vmem_limit_bytes=4 * 1024 * 1024),
        name="combine",
    )(*args)


def shards(tokens, expert_ids, route_weight, gate_weight, up_weight, down_weight):
    ctx_size = lax.axis_size("ctx")
    tp_size = lax.axis_size("tp")
    groups = tp_size // SPLIT
    chips = tp_size // CORES
    tok_rows, features = tokens.shape
    slots = groups * CAP
    rows = ctx_size * CAP
    units = gate_weight.shape[1]

    def over_ctx(array, mask):
        return lax.ppermute(array, "ctx", swaps(ctx_size, mask))

    def over_chips(array, mask):
        return lax.ppermute(array, "tp", swaps(tp_size, mask * CORES))

    def over_cores(array):
        return lax.ppermute(array, "tp", swaps(tp_size, 1))

    weights, *picked = route(expert_ids.T, route_weight.T, tokens, ctx_size, groups)
    masks = turns(ctx_size)
    half = ctx_size // 2
    gate, mix = load_gate(gate_weight, weights)
    blocks = [over_ctx(p, mask) if mask else p for p, mask in zip(picked, masks)]
    chip = lax.axis_index("tp") // CORES

    def stacked(mask, part, after):
        pieces = blocks[part]
        if groups > 1:
            group = (chip ^ mask) // (chips // groups)
            pieces = [lax.dynamic_slice_in_dim(p, group * CAP, CAP) for p in pieces]
        return stack(pieces, "stack_half", after)

    halves = (slice(half, ctx_size), slice(0, half))
    mine = [stacked(0, halves[0], ())]
    mark = local(
        mark_kernel, "mark", sds((8, 128), F32), (mine[0],), unread=(0,), cost=2**24
    )
    mine.append(stacked(0, halves[1], (mark, gate)))
    arriving = [
        [
            over_chips(mine[i] if groups == 1 else stacked(j, part, (mine[i],)), j)
            for i, part in enumerate(halves)
        ]
        for j in range(1, chips)
    ]
    near = [stack(mine, "stack_own", (), (1, 0))]
    far = [over_cores(near[0])]
    up, *part = load_up(near[0], gate, up_weight)
    down = pltpu.with_memory_space_constraint(down_weight[0], pltpu.VMEM)
    near += [stack(pair, "stack_near", (up, down), (1, 0)) for pair in arriving]
    far += [over_cores(chunk) for chunk in near[1:]]
    part = local(
        functools.partial(grow_kernel, [1] + [j * CORES for j in range(1, chips)]),
        "grow",
        [sds((units, rows), F32)] * 2,
        (far[0], *near[1:], gate, up, *part),
    )
    away = [j * CORES for j in range(1, chips)]
    hidden, given = local(
        functools.partial(expert_kernel, [m + 1 for m in away], [m + 1 for m in away]),
        "expert",
        [sds((rows, units)), sds((len(away) * rows, features))],
        (*far[1:], gate, up, down, *part),
    )

    def shrunk(masks, name, after=()):
        return local(
            functools.partial(shrink_kernel, masks),
            name,
            sds((len(masks) * rows, features)),
            (hidden, down, *after),
            unread=range(2, 2 + len(after)),
        )

    other_away = over_cores(given)
    own_away = shrunk(away, "own_away")
    leaving = local(
        functools.partial(pair_kernel, rows),
        "pair",
        [sds((rows - CAP, features))] * (chips - 1),
        (own_away, other_away),
    )
    parts = [over_chips(leaving[j - 1], j) for j in range(1, chips)]
    given = shrunk([1], "given", (own_away,))
    own = shrunk([0], "own", (given,))
    other = over_cores(stack((given,), "stack_given", (own, other_away)))
    tail = local(
        tail_kernel, "tail", sds((chips * CAP, features)), (own, other, own_away, other_away)
    )
    got = over_ctx(tail, masks[-1])
    sums = local(
        functools.partial(total_kernel, groups, chips),
        "total",
        [sds((slots, features))] * (ctx_size - 1),
        (own, other, *parts),
    )
    far_first = sorted(zip(masks, sums), key=lambda pair: -pair[0])
    backs = [over_ctx(p, turn) if turn else p for turn, p in far_first]
    place = {turn: i for i, (turn, _) in enumerate(far_first)}
    order = [place[turn] for turn in masks[:-1]]
    pieces = local(split_kernel, "split", [sds((CAP, features))] * chips, (got,))
    late = [pieces[0]] + [over_chips(pieces[j], j) for j in range(1, chips)]
    return combine(mix, order, groups, backs, late)


def solution(mesh):
    return jax.shard_map(
        shards,
        mesh=mesh,
        in_specs=(
            P(("dp", "ctx"), "tp"),
            P(("dp", "ctx"), None),
            P(("dp", "ctx"), None),
            P(("ctx", "tp"), None, None),
            P(("ctx", "tp"), None, None),
            P(("ctx", "tp"), None, None),
        ),
        out_specs=P(("dp", "ctx"), "tp"),
        check_vma=False,
    )
```

```python
import functools

import jax
import jax.numpy as jnp
from jax import lax
from jax.experimental import pallas as pl
from jax.experimental.pallas import tpu as pltpu
from jax.sharding import PartitionSpec as P

SPLIT = 4
CAP = 16
CORES = 2
F32 = jnp.float32
BF16 = jnp.bfloat16
VMEM = pl.BlockSpec(memory_space=pltpu.VMEM)
HBM = pl.BlockSpec(memory_space=pltpu.HBM)
NT = (((1,), (1,)), ((), ()))


def swaps(size, mask):
    return [(i, i ^ mask) for i in range(size)]


def turns(size):
    half = size // 2
    return [*range(size - 1, half, -1), *range(1, half), 0, half]


def sds(shape, dtype=BF16):
    return jax.ShapeDtypeStruct(shape, dtype)


def local(kernel, name, out_shape, args, unread=(), cost=0):
    specs = [pl.BlockSpec(memory_space=pl.ANY) if i in unread else VMEM for i in range(len(args))]
    moved = cost or sum(a.size * a.dtype.itemsize for a in args)
    return pl.pallas_call(
        kernel,
        out_shape=out_shape,
        in_specs=specs,
        out_specs=jax.tree.map(lambda _: VMEM, out_shape),
        compiler_params=pltpu.CompilerParams(vmem_limit_bytes=4 * 1024 * 1024),
        cost_estimate=pl.CostEstimate(flops=0, bytes_accessed=moved, transcendentals=0),
        name=name,
    )(*args)


def columns(mask, features):
    at = lax.axis_index("tp") ^ mask
    return pl.ds(pl.multiple_of(at * features, features), features)


def route_kernel(ctx_size, groups, ids_hbm, weight_hbm, tokens_hbm, combine_ref, *refs):
    *row_refs, ids_ref, weight_ref, tokens_ref, sems = refs
    copies = [
        pltpu.make_async_copy(source, target, sems.at[i])
        for i, (source, target) in enumerate(
            ((ids_hbm, ids_ref), (weight_hbm, weight_ref), (tokens_hbm, tokens_ref))
        )
    ]
    for copy in copies:
        copy.start()
    slots = groups * CAP
    top, tok_rows = ids_ref.shape
    places = ctx_size * slots
    here = lax.axis_index("ctx")
    place = lax.broadcasted_iota(jnp.int32, (places, tok_rows), 0)
    order = place // slots
    turn = jnp.zeros_like(place)
    for i, mask in enumerate(turns(ctx_size)):
        turn = jnp.where(order == i, mask, turn)
    expert = (turn ^ here) * groups + (place % slots) // CAP
    slot = (place % CAP).astype(F32)
    before = (
        lax.broadcasted_iota(jnp.int32, (tok_rows, tok_rows), 0)
        < lax.broadcasted_iota(jnp.int32, (tok_rows, tok_rows), 1)
    ).astype(BF16)
    member = jnp.zeros((places, tok_rows), F32)
    weight = jnp.zeros((places, tok_rows), F32)
    copies[0].wait()
    copies[1].wait()
    for k in range(top):
        hit = ids_ref[k : k + 1, :] == expert
        member = jnp.where(hit, 1.0, member)
        weight = jnp.where(hit, weight_ref[k : k + 1, :], weight)
    running = jnp.dot(member.astype(BF16), before, preferred_element_type=F32)
    picked = jnp.where(running == slot, member, 0.0)
    combine_ref[...] = picked * weight
    copies[2].wait()
    rows = jnp.dot(picked.astype(BF16), tokens_ref[...], preferred_element_type=F32).astype(BF16)
    for s, ref in enumerate(row_refs):
        ref[...] = rows[s * slots : (s + 1) * slots]


def route(ids_t, weight_t, tokens, ctx_size, groups):
    tok_rows, features = tokens.shape
    slots = groups * CAP
    args = (ids_t, weight_t, tokens)
    return pl.pallas_call(
        functools.partial(route_kernel, ctx_size, groups),
        out_shape=[sds((ctx_size * slots, tok_rows), F32)] + [sds((slots, features))] * ctx_size,
        in_specs=[HBM] * 3,
        out_specs=[VMEM] * (ctx_size + 1),
        scratch_shapes=[pltpu.VMEM(a.shape, a.dtype) for a in args]
        + [pltpu.SemaphoreType.DMA((3,))],
        compiler_params=pltpu.CompilerParams(vmem_limit_bytes=4 * 1024 * 1024),
        name="route",
    )(*[pltpu.with_memory_space_constraint(a, pltpu.HBM) for a in args])


def load_gate_kernel(cuts, gate_hbm, combine_ref, both_ref, mix_ref, sems):
    step = gate_hbm.shape[1] // cuts
    copies = []
    for c in range(cuts):
        part = pl.ds(c * step, step)
        copies.append(pltpu.make_async_copy(gate_hbm.at[0, part], both_ref.at[part], sems.at[c]))
    for copy in copies:
        copy.start()
    weight = combine_ref[...].T
    high = weight.astype(BF16)
    mix_ref[...] = jnp.concatenate([high, (weight - high.astype(F32)).astype(BF16)], axis=1)
    for copy in copies:
        copy.wait()


def load_gate(gate_weight, weights, cuts=4):
    places, tok_rows = weights.shape
    _, units, width = gate_weight.shape
    return pl.pallas_call(
        functools.partial(load_gate_kernel, cuts),
        out_shape=[sds((2 * units, width)), sds((tok_rows, 2 * places))],
        in_specs=[HBM, VMEM],
        out_specs=[VMEM] * 2,
        scratch_shapes=[pltpu.SemaphoreType.DMA((cuts,))],
        compiler_params=pltpu.CompilerParams(vmem_limit_bytes=12 * 1024 * 1024),
        cost_estimate=pl.CostEstimate(
            flops=0, bytes_accessed=4 * gate_weight.size, transcendentals=0
        ),
        name="load_gate",
    )(pltpu.with_memory_space_constraint(gate_weight, pltpu.HBM), weights)


def mark_kernel(_, out_ref):
    out_ref[...] = jnp.zeros(out_ref.shape, F32)


def load_up_kernel(x_ref, _, up_hbm, both_ref, sums_out, sems):
    features = x_ref.shape[1]
    units = up_hbm.shape[1]
    copies = []
    for mask in range(both_ref.shape[1] // features):
        part = columns(mask, features)
        copies.append(
            pltpu.make_async_copy(
                up_hbm.at[0, :, part], both_ref.at[units:, part], sems.at[mask]
            )
        )
    for copy in copies:
        copy.start()
    x = x_ref[...]
    own = columns(0, features)
    sums_out[:units, :] = lax.dot_general(
        both_ref[:units, own], x, NT, preferred_element_type=F32
    )
    copies[0].wait()
    sums_out[units:, :] = lax.dot_general(
        both_ref[units:, own], x, NT, preferred_element_type=F32
    )
    for copy in copies[1:]:
        copy.wait()


def load_up(x, both, up_weight):
    rows, features = x.shape
    units, width = both.shape
    return pl.pallas_call(
        load_up_kernel,
        out_shape=[sds((units, width)), sds((units, rows), F32)],
        in_specs=[VMEM, VMEM, HBM],
        out_specs=[VMEM] * 2,
        input_output_aliases={1: 0},
        scratch_shapes=[pltpu.SemaphoreType.DMA((width // features,))],
        compiler_params=pltpu.CompilerParams(vmem_limit_bytes=20 * 1024 * 1024),
        cost_estimate=pl.CostEstimate(
            flops=0, bytes_accessed=4 * up_weight.size, transcendentals=0
        ),
        name="load_up",
    )(
        x,
        pltpu.with_memory_space_constraint(both, pltpu.VMEM),
        pltpu.with_memory_space_constraint(up_weight, pltpu.HBM),
    )


def stack_kernel(places, *refs):
    out_ref = refs[-1]
    for place, ref in zip(places, refs[-1 - len(places) : -1]):
        out_ref[place * ref.shape[0] : (place + 1) * ref.shape[0], :] = ref[...]


def stack(pieces, name, after, places=None):
    places = places or list(range(len(pieces)))
    rows = len(pieces) * pieces[0].shape[0]
    return local(
        functools.partial(stack_kernel, places),
        name,
        sds((rows, pieces[0].shape[1])),
        (*after, *pieces),
        unread=range(len(after)),
    )


def grow(chunks, masks, both_ref, sums):
    for ref, mask in zip(chunks, masks):
        own = columns(mask, ref.shape[1])
        sums = sums + lax.dot_general(both_ref[:, own], ref[...], NT, preferred_element_type=F32)
    return sums


def grow_kernel(masks, *refs):
    chunks, (both_ref, sums_in, sums_out) = refs[:-3], refs[-3:]
    sums_out[...] = grow(chunks, masks, both_ref, sums_in[...])


def expert_kernel(masks, out_masks, *refs):
    chunks = refs[: len(masks)]
    both_ref, down_ref, sums_in, hidden_ref, out_ref = refs[len(masks) :]
    sums = grow(chunks, masks, both_ref, sums_in[...])
    units = sums.shape[0] // 2
    gate_vals, up_vals = sums[:units], sums[units:]
    hidden = (gate_vals / (1.0 + jnp.exp(-gate_vals)) * up_vals).T.astype(BF16)
    hidden_ref[...] = hidden
    shrink(hidden, out_masks, down_ref, out_ref)


def shrink(hidden, masks, down_ref, out_ref):
    rows, features = hidden.shape[0], out_ref.shape[1]
    for i, mask in enumerate(masks):
        down = down_ref[:, columns(mask, features)]
        out = jnp.dot(hidden, down, preferred_element_type=F32)
        out_ref[i * rows : (i + 1) * rows, :] = out.astype(BF16)


def shrink_kernel(masks, hidden_ref, down_ref, *refs):
    out_ref = refs[-1]
    shrink(hidden_ref[...], masks, down_ref, out_ref)


def pair_kernel(rows, own_ref, other_ref, *out_refs):
    count = out_refs[0].shape[0]
    for j, ref in enumerate(out_refs):
        at = slice(j * rows, j * rows + count)
        ref[...] = (own_ref[at, :].astype(F32) + other_ref[at, :].astype(F32)).astype(BF16)


def tail_kernel(own_ref, other_ref, own_away_ref, other_away_ref, out_ref):
    rows = own_ref.shape[0]
    for j in range(out_ref.shape[0] // CAP):
        mine, others = (own_ref, other_ref) if j == 0 else (own_away_ref, other_away_ref)
        at = slice(max(j, 1) * rows - CAP, max(j, 1) * rows)
        total = mine[at, :].astype(F32) + others[at, :].astype(F32)
        out_ref[j * CAP : (j + 1) * CAP, :] = total.astype(BF16)


def split_kernel(in_ref, *out_refs):
    for j, ref in enumerate(out_refs):
        ref[...] = in_ref[j * CAP : (j + 1) * CAP, :]


def group_sums(groups, parts):
    chips = len(parts)
    chip = lax.axis_index("tp") // CORES
    per_group = chips // groups
    totals = []
    for g in range(groups):
        total = None
        for j, term in enumerate(parts):
            if groups > 1:
                term = jnp.where((chip ^ j) // per_group == g, term, 0.0)
            total = term if total is None else total + term
        totals.append(total.astype(BF16))
    return totals


def total_kernel(groups, chips, own_ref, other_ref, *refs):
    part_refs, out_refs = refs[: chips - 1], refs[chips - 1 :]
    count = part_refs[0].shape[0]
    parts = [own_ref[:count, :].astype(F32) + other_ref[:count, :].astype(F32)]
    parts += [ref[...].astype(F32) for ref in part_refs]
    for g, total in enumerate(group_sums(groups, parts)):
        for s, ref in enumerate(out_refs):
            ref[g * CAP : (g + 1) * CAP, :] = total[s * CAP : (s + 1) * CAP]


def combine_kernel(order, groups, cuts, mix_ref, *refs):
    out_hbm, out_ref, sems = refs[-3:]
    count = len(order)
    back_refs, part_refs = refs[:count], refs[count:-3]
    back_refs = [back_refs[i] for i in order]
    mix = mix_ref[...]
    step = out_ref.shape[1] // cuts
    copies = []
    for c in range(cuts):
        part = slice(c * step, (c + 1) * step)
        parts = [ref[:, part].astype(F32) for ref in part_refs]
        back = [ref[:, part] for ref in back_refs] + group_sums(groups, parts)
        back = jnp.concatenate(back * 2, axis=0)
        out_ref[:, part] = jnp.dot(mix, back, preferred_element_type=F32).astype(BF16)
        copies.append(
            pltpu.make_async_copy(out_ref.at[:, part], out_hbm.at[:, part], sems.at[c])
        )
        copies[c].start()
    for copy in copies:
        copy.wait()


def combine(mix, order, groups, backs, parts, cuts=2):
    shape = sds((mix.shape[0], backs[0].shape[1]))
    args = (mix, *backs, *parts)
    return pl.pallas_call(
        functools.partial(combine_kernel, order, groups, cuts),
        out_shape=shape,
        in_specs=[VMEM] * len(args),
        out_specs=HBM,
        scratch_shapes=[pltpu.VMEM(shape.shape, BF16), pltpu.SemaphoreType.DMA((cuts,))],
        compiler_params=pltpu.CompilerParams(vmem_limit_bytes=4 * 1024 * 1024),
        name="combine",
    )(*args)


def shards(tokens, expert_ids, route_weight, gate_weight, up_weight, down_weight):
    ctx_size = lax.axis_size("ctx")
    tp_size = lax.axis_size("tp")
    groups = tp_size // SPLIT
    chips = tp_size // CORES
    tok_rows, features = tokens.shape
    slots = groups * CAP
    rows = ctx_size * CAP
    units = gate_weight.shape[1]

    def over_ctx(array, mask):
        return lax.ppermute(array, "ctx", swaps(ctx_size, mask))

    def over_chips(array, mask):
        return lax.ppermute(array, "tp", swaps(tp_size, mask * CORES))

    def over_cores(array):
        return lax.ppermute(array, "tp", swaps(tp_size, 1))

    weights, *picked = route(expert_ids.T, route_weight.T, tokens, ctx_size, groups)
    masks = turns(ctx_size)
    half = ctx_size // 2
    gate, mix = load_gate(gate_weight, weights)
    blocks = [over_ctx(p, mask) if mask else p for p, mask in zip(picked, masks)]
    chip = lax.axis_index("tp") // CORES

    def stacked(mask, part, after):
        pieces = blocks[part]
        if groups > 1:
            group = (chip ^ mask) // (chips // groups)
            pieces = [lax.dynamic_slice_in_dim(p, group * CAP, CAP) for p in pieces]
        return stack(pieces, "stack_half", after)

    halves = (slice(half, ctx_size), slice(0, half))
    mine = [stacked(0, halves[0], ())]
    mark = local(
        mark_kernel, "mark", sds((8, 128), F32), (mine[0],), unread=(0,), cost=2**24
    )
    mine.append(stacked(0, halves[1], (mark, gate)))
    arriving = [
        [
            over_chips(mine[i] if groups == 1 else stacked(j, part, (mine[i],)), j)
            for i, part in enumerate(halves)
        ]
        for j in range(1, chips)
    ]
    near = [stack(mine, "stack_own", (), (1, 0))]
    far = [over_cores(near[0])]
    both, part = load_up(near[0], gate, up_weight)
    down = pltpu.with_memory_space_constraint(down_weight[0], pltpu.VMEM)
    near += [stack(pair, "stack_near", (both, down), (1, 0)) for pair in arriving]
    far += [over_cores(chunk) for chunk in near[1:]]
    part = local(
        functools.partial(grow_kernel, [1] + [j * CORES for j in range(1, chips)]),
        "grow",
        sds((2 * units, rows), F32),
        (far[0], *near[1:], both, part),
    )
    away = [j * CORES for j in range(1, chips)]
    hidden, given = local(
        functools.partial(expert_kernel, [m + 1 for m in away], [m + 1 for m in away]),
        "expert",
        [sds((rows, units)), sds((len(away) * rows, features))],
        (*far[1:], both, down, part),
    )

    def shrunk(masks, name, after=()):
        return local(
            functools.partial(shrink_kernel, masks),
            name,
            sds((len(masks) * rows, features)),
            (hidden, down, *after),
            unread=range(2, 2 + len(after)),
        )

    other_away = over_cores(given)
    own_away = shrunk(away, "own_away")
    leaving = local(
        functools.partial(pair_kernel, rows),
        "pair",
        [sds((rows - CAP, features))] * (chips - 1),
        (own_away, other_away),
    )
    parts = [over_chips(leaving[j - 1], j) for j in range(1, chips)]
    given = shrunk([1], "given", (own_away,))
    own = shrunk([0], "own", (given,))
    other = over_cores(stack((given,), "stack_given", (own, other_away)))
    tail = local(
        tail_kernel, "tail", sds((chips * CAP, features)), (own, other, own_away, other_away)
    )
    got = over_ctx(tail, masks[-1])
    sums = local(
        functools.partial(total_kernel, groups, chips),
        "total",
        [sds((slots, features))] * (ctx_size - 1),
        (own, other, *parts),
    )
    far_first = sorted(zip(masks, sums), key=lambda pair: -pair[0])
    backs = [over_ctx(p, turn) if turn else p for turn, p in far_first]
    place = {turn: i for i, (turn, _) in enumerate(far_first)}
    order = [place[turn] for turn in masks[:-1]]
    pieces = local(split_kernel, "split", [sds((CAP, features))] * chips, (got,))
    late = [pieces[0]] + [over_chips(pieces[j], j) for j in range(1, chips)]
    return combine(mix, order, groups, backs, late)


def solution(mesh):
    return jax.shard_map(
        shards,
        mesh=mesh,
        in_specs=(
            P(("dp", "ctx"), "tp"),
            P(("dp", "ctx"), None),
            P(("dp", "ctx"), None),
            P(("ctx", "tp"), None, None),
            P(("ctx", "tp"), None, None),
            P(("ctx", "tp"), None, None),
        ),
        out_specs=P(("dp", "ctx"), "tp"),
        check_vma=False,
    )
```

```python
import functools

import jax
import jax.numpy as jnp
from jax import lax
from jax.experimental import pallas as pl
from jax.experimental.pallas import tpu as pltpu
from jax.sharding import PartitionSpec as P

SPLIT = 4
CAP = 16
CORES = 2
F32 = jnp.float32
BF16 = jnp.bfloat16
VMEM = pl.BlockSpec(memory_space=pltpu.VMEM)
HBM = pl.BlockSpec(memory_space=pltpu.HBM)
NT = (((1,), (1,)), ((), ()))


def swaps(size, mask):
    return [(i, i ^ mask) for i in range(size)]


def turns(size):
    half = size // 2
    return [*range(size - 1, half, -1), *range(1, half), 0, half]


def sds(shape, dtype=BF16):
    return jax.ShapeDtypeStruct(shape, dtype)


def local(kernel, name, out_shape, args, unread=(), cost=0):
    specs = [pl.BlockSpec(memory_space=pl.ANY) if i in unread else VMEM for i in range(len(args))]
    moved = cost or sum(a.size * a.dtype.itemsize for a in args)
    return pl.pallas_call(
        kernel,
        out_shape=out_shape,
        in_specs=specs,
        out_specs=jax.tree.map(lambda _: VMEM, out_shape),
        compiler_params=pltpu.CompilerParams(vmem_limit_bytes=4 * 1024 * 1024),
        cost_estimate=pl.CostEstimate(flops=0, bytes_accessed=moved, transcendentals=0),
        name=name,
    )(*args)


def columns(mask, features):
    at = lax.axis_index("tp") ^ mask
    return pl.ds(pl.multiple_of(at * features, features), features)


def route_kernel(ctx_size, groups, cuts, ids_hbm, weight_hbm, tokens_hbm, combine_ref, *refs):
    *row_refs, ids_ref, weight_ref, tokens_ref, sems = refs
    copies = [
        pltpu.make_async_copy(source, target, sems.at[i])
        for i, (source, target) in enumerate(((ids_hbm, ids_ref), (weight_hbm, weight_ref)))
    ]
    step = tokens_ref.shape[0] // cuts
    for c in range(cuts):
        part = pl.ds(c * step, step)
        copies.append(
            pltpu.make_async_copy(tokens_hbm.at[part], tokens_ref.at[part], sems.at[2 + c])
        )
    for copy in copies:
        copy.start()
    slots = groups * CAP
    top, tok_rows = ids_ref.shape
    places = ctx_size * slots
    here = lax.axis_index("ctx")
    place = lax.broadcasted_iota(jnp.int32, (places, tok_rows), 0)
    order = place // slots
    turn = jnp.zeros_like(place)
    for i, mask in enumerate(turns(ctx_size)):
        turn = jnp.where(order == i, mask, turn)
    expert = (turn ^ here) * groups + (place % slots) // CAP
    slot = (place % CAP).astype(F32)
    before = (
        lax.broadcasted_iota(jnp.int32, (tok_rows, tok_rows), 0)
        < lax.broadcasted_iota(jnp.int32, (tok_rows, tok_rows), 1)
    ).astype(BF16)
    member = jnp.zeros((places, tok_rows), F32)
    weight = jnp.zeros((places, tok_rows), F32)
    copies[0].wait()
    copies[1].wait()
    for k in range(top):
        hit = ids_ref[k : k + 1, :] == expert
        member = jnp.where(hit, 1.0, member)
        weight = jnp.where(hit, weight_ref[k : k + 1, :], weight)
    running = jnp.dot(member.astype(BF16), before, preferred_element_type=F32)
    picked = jnp.where(running == slot, member, 0.0)
    combine_ref[...] = picked * weight
    for copy in copies[2:]:
        copy.wait()
    rows = jnp.dot(picked.astype(BF16), tokens_ref[...], preferred_element_type=F32).astype(BF16)
    for s, ref in enumerate(row_refs):
        ref[...] = rows[s * slots : (s + 1) * slots]


def route(ids_t, weight_t, tokens, ctx_size, groups, cuts=4):
    tok_rows, features = tokens.shape
    slots = groups * CAP
    args = (ids_t, weight_t, tokens)
    return pl.pallas_call(
        functools.partial(route_kernel, ctx_size, groups, cuts),
        out_shape=[sds((ctx_size * slots, tok_rows), F32)] + [sds((slots, features))] * ctx_size,
        in_specs=[HBM] * 3,
        out_specs=[VMEM] * (ctx_size + 1),
        scratch_shapes=[pltpu.VMEM(a.shape, a.dtype) for a in args]
        + [pltpu.SemaphoreType.DMA((2 + cuts,))],
        compiler_params=pltpu.CompilerParams(vmem_limit_bytes=4 * 1024 * 1024),
        name="route",
    )(*[pltpu.with_memory_space_constraint(a, pltpu.HBM) for a in args])


def load_gate_kernel(cuts, gate_hbm, combine_ref, both_ref, mix_ref, sems):
    step = gate_hbm.shape[1] // cuts
    copies = []
    for c in range(cuts):
        part = pl.ds(c * step, step)
        copies.append(pltpu.make_async_copy(gate_hbm.at[0, part], both_ref.at[part], sems.at[c]))
    for copy in copies:
        copy.start()
    weight = combine_ref[...].T
    high = weight.astype(BF16)
    mix_ref[...] = jnp.concatenate([high, (weight - high.astype(F32)).astype(BF16)], axis=1)
    for copy in copies:
        copy.wait()


def load_gate(gate_weight, weights, cuts=4):
    places, tok_rows = weights.shape
    _, units, width = gate_weight.shape
    return pl.pallas_call(
        functools.partial(load_gate_kernel, cuts),
        out_shape=[sds((2 * units, width)), sds((tok_rows, 2 * places))],
        in_specs=[HBM, VMEM],
        out_specs=[VMEM] * 2,
        scratch_shapes=[pltpu.SemaphoreType.DMA((cuts,))],
        compiler_params=pltpu.CompilerParams(vmem_limit_bytes=12 * 1024 * 1024),
        cost_estimate=pl.CostEstimate(
            flops=0, bytes_accessed=4 * gate_weight.size, transcendentals=0
        ),
        name="load_gate",
    )(pltpu.with_memory_space_constraint(gate_weight, pltpu.HBM), weights)


def mark_kernel(_, out_ref):
    out_ref[...] = jnp.zeros(out_ref.shape, F32)


def load_up_kernel(x_ref, _, up_hbm, both_ref, sums_out, sems):
    features = x_ref.shape[1]
    units = up_hbm.shape[1]
    copies = []
    for mask in range(both_ref.shape[1] // features):
        part = columns(mask, features)
        copies.append(
            pltpu.make_async_copy(
                up_hbm.at[0, :, part], both_ref.at[units:, part], sems.at[mask]
            )
        )
    for copy in copies:
        copy.start()
    x = x_ref[...]
    own = columns(0, features)
    sums_out[:units, :] = lax.dot_general(
        both_ref[:units, own], x, NT, preferred_element_type=F32
    )
    copies[0].wait()
    sums_out[units:, :] = lax.dot_general(
        both_ref[units:, own], x, NT, preferred_element_type=F32
    )
    for copy in copies[1:]:
        copy.wait()


def load_up(x, both, up_weight):
    rows, features = x.shape
    units, width = both.shape
    return pl.pallas_call(
        load_up_kernel,
        out_shape=[sds((units, width)), sds((units, rows), F32)],
        in_specs=[VMEM, VMEM, HBM],
        out_specs=[VMEM] * 2,
        input_output_aliases={1: 0},
        scratch_shapes=[pltpu.SemaphoreType.DMA((width // features,))],
        compiler_params=pltpu.CompilerParams(vmem_limit_bytes=20 * 1024 * 1024),
        cost_estimate=pl.CostEstimate(
            flops=0, bytes_accessed=4 * up_weight.size, transcendentals=0
        ),
        name="load_up",
    )(
        x,
        pltpu.with_memory_space_constraint(both, pltpu.VMEM),
        pltpu.with_memory_space_constraint(up_weight, pltpu.HBM),
    )


def stack_kernel(places, *refs):
    out_ref = refs[-1]
    for place, ref in zip(places, refs[-1 - len(places) : -1]):
        out_ref[place * ref.shape[0] : (place + 1) * ref.shape[0], :] = ref[...]


def stack(pieces, name, after, places=None):
    places = places or list(range(len(pieces)))
    rows = len(pieces) * pieces[0].shape[0]
    return local(
        functools.partial(stack_kernel, places),
        name,
        sds((rows, pieces[0].shape[1])),
        (*after, *pieces),
        unread=range(len(after)),
    )


def grow(chunks, masks, both_ref, sums):
    for ref, mask in zip(chunks, masks):
        own = columns(mask, ref.shape[1])
        sums = sums + lax.dot_general(both_ref[:, own], ref[...], NT, preferred_element_type=F32)
    return sums


def grow_kernel(masks, *refs):
    chunks, (both_ref, sums_in, sums_out) = refs[:-3], refs[-3:]
    sums_out[...] = grow(chunks, masks, both_ref, sums_in[...])


def expert_kernel(masks, out_masks, *refs):
    chunks = refs[: len(masks)]
    both_ref, down_ref, sums_in, hidden_ref, out_ref = refs[len(masks) :]
    sums = grow(chunks, masks, both_ref, sums_in[...])
    units = sums.shape[0] // 2
    gate_vals, up_vals = sums[:units], sums[units:]
    hidden = (gate_vals / (1.0 + jnp.exp(-gate_vals)) * up_vals).T.astype(BF16)
    hidden_ref[...] = hidden
    shrink(hidden, out_masks, down_ref, out_ref)


def shrink(hidden, masks, down_ref, out_ref):
    rows, features = hidden.shape[0], out_ref.shape[1]
    for i, mask in enumerate(masks):
        down = down_ref[:, columns(mask, features)]
        out = jnp.dot(hidden, down, preferred_element_type=F32)
        out_ref[i * rows : (i + 1) * rows, :] = out.astype(BF16)


def shrink_kernel(masks, hidden_ref, down_ref, *refs):
    out_ref = refs[-1]
    shrink(hidden_ref[...], masks, down_ref, out_ref)


def pair_kernel(rows, own_ref, other_ref, *out_refs):
    count = out_refs[0].shape[0]
    for j, ref in enumerate(out_refs):
        at = slice(j * rows, j * rows + count)
        ref[...] = (own_ref[at, :].astype(F32) + other_ref[at, :].astype(F32)).astype(BF16)


def tail_kernel(own_ref, other_ref, own_away_ref, other_away_ref, out_ref):
    rows = own_ref.shape[0]
    for j in range(out_ref.shape[0] // CAP):
        mine, others = (own_ref, other_ref) if j == 0 else (own_away_ref, other_away_ref)
        at = slice(max(j, 1) * rows - CAP, max(j, 1) * rows)
        total = mine[at, :].astype(F32) + others[at, :].astype(F32)
        out_ref[j * CAP : (j + 1) * CAP, :] = total.astype(BF16)


def split_kernel(in_ref, *out_refs):
    for j, ref in enumerate(out_refs):
        ref[...] = in_ref[j * CAP : (j + 1) * CAP, :]


def group_sums(groups, parts):
    chips = len(parts)
    chip = lax.axis_index("tp") // CORES
    per_group = chips // groups
    totals = []
    for g in range(groups):
        total = None
        for j, term in enumerate(parts):
            if groups > 1:
                term = jnp.where((chip ^ j) // per_group == g, term, 0.0)
            total = term if total is None else total + term
        totals.append(total.astype(BF16))
    return totals


def total_kernel(groups, chips, own_ref, other_ref, *refs):
    part_refs, out_refs = refs[: chips - 1], refs[chips - 1 :]
    count = part_refs[0].shape[0]
    parts = [own_ref[:count, :].astype(F32) + other_ref[:count, :].astype(F32)]
    parts += [ref[...].astype(F32) for ref in part_refs]
    for g, total in enumerate(group_sums(groups, parts)):
        for s, ref in enumerate(out_refs):
            ref[g * CAP : (g + 1) * CAP, :] = total[s * CAP : (s + 1) * CAP]


def combine_kernel(order, groups, cuts, mix_ref, *refs):
    out_hbm, out_ref, sems = refs[-3:]
    count = len(order)
    back_refs, part_refs = refs[:count], refs[count:-3]
    back_refs = [back_refs[i] for i in order]
    late = group_sums(groups, [ref[...].astype(F32) for ref in part_refs])
    back = jnp.concatenate([*[ref[...] for ref in back_refs], *late] * 2, axis=0)
    step = out_ref.shape[0] // cuts
    copies = []
    for c in range(cuts):
        part = slice(c * step, (c + 1) * step)
        out = jnp.dot(mix_ref[part, :], back, preferred_element_type=F32)
        out_ref[part, :] = out.astype(BF16)
        copies.append(pltpu.make_async_copy(out_ref.at[part], out_hbm.at[part], sems.at[c]))
        copies[c].start()
    for copy in copies:
        copy.wait()


def combine(mix, order, groups, backs, parts, cuts=2):
    shape = sds((mix.shape[0], backs[0].shape[1]))
    args = (mix, *backs, *parts)
    return pl.pallas_call(
        functools.partial(combine_kernel, order, groups, cuts),
        out_shape=shape,
        in_specs=[VMEM] * len(args),
        out_specs=HBM,
        scratch_shapes=[pltpu.VMEM(shape.shape, BF16), pltpu.SemaphoreType.DMA((cuts,))],
        compiler_params=pltpu.CompilerParams(vmem_limit_bytes=4 * 1024 * 1024),
        name="combine",
    )(*args)


def shards(tokens, expert_ids, route_weight, gate_weight, up_weight, down_weight):
    ctx_size = lax.axis_size("ctx")
    tp_size = lax.axis_size("tp")
    groups = tp_size // SPLIT
    chips = tp_size // CORES
    tok_rows, features = tokens.shape
    slots = groups * CAP
    rows = ctx_size * CAP
    units = gate_weight.shape[1]

    def over_ctx(array, mask):
        return lax.ppermute(array, "ctx", swaps(ctx_size, mask))

    def over_chips(array, mask):
        return lax.ppermute(array, "tp", swaps(tp_size, mask * CORES))

    def over_cores(array):
        return lax.ppermute(array, "tp", swaps(tp_size, 1))

    weights, *picked = route(expert_ids.T, route_weight.T, tokens, ctx_size, groups)
    masks = turns(ctx_size)
    half = ctx_size // 2
    gate, mix = load_gate(gate_weight, weights)
    blocks = [over_ctx(p, mask) if mask else p for p, mask in zip(picked, masks)]
    chip = lax.axis_index("tp") // CORES

    def stacked(mask, part, after):
        pieces = blocks[part]
        if groups > 1:
            group = (chip ^ mask) // (chips // groups)
            pieces = [lax.dynamic_slice_in_dim(p, group * CAP, CAP) for p in pieces]
        return stack(pieces, "stack_half", after)

    halves = (slice(half, ctx_size), slice(0, half))
    mine = [stacked(0, halves[0], ())]
    mark = local(
        mark_kernel, "mark", sds((8, 128), F32), (mine[0],), unread=(0,), cost=2**24
    )
    mine.append(stacked(0, halves[1], (mark, gate)))
    arriving = [
        [
            over_chips(mine[i] if groups == 1 else stacked(j, part, (mine[i],)), j)
            for i, part in enumerate(halves)
        ]
        for j in range(1, chips)
    ]
    near = [stack(mine, "stack_own", (), (1, 0))]
    far = [over_cores(near[0])]
    both, part = load_up(near[0], gate, up_weight)
    down = pltpu.with_memory_space_constraint(down_weight[0], pltpu.VMEM)
    near += [stack(pair, "stack_near", (both, down), (1, 0)) for pair in arriving]
    far += [over_cores(chunk) for chunk in near[1:]]
    part = local(
        functools.partial(grow_kernel, [1] + [j * CORES for j in range(1, chips)]),
        "grow",
        sds((2 * units, rows), F32),
        (far[0], *near[1:], both, part),
    )
    away = [j * CORES for j in range(1, chips)]
    hidden, given = local(
        functools.partial(expert_kernel, [m + 1 for m in away], [m + 1 for m in away]),
        "expert",
        [sds((rows, units)), sds((len(away) * rows, features))],
        (*far[1:], both, down, part),
    )

    def shrunk(masks, name, after=()):
        return local(
            functools.partial(shrink_kernel, masks),
            name,
            sds((len(masks) * rows, features)),
            (hidden, down, *after),
            unread=range(2, 2 + len(after)),
        )

    other_away = over_cores(given)
    own_away = shrunk(away, "own_away")
    leaving = local(
        functools.partial(pair_kernel, rows),
        "pair",
        [sds((rows - CAP, features))] * (chips - 1),
        (own_away, other_away),
    )
    parts = [over_chips(leaving[j - 1], j) for j in range(1, chips)]
    given = shrunk([1], "given", (own_away,))
    own = shrunk([0], "own", (given,))
    other = over_cores(stack((given,), "stack_given", (own, other_away)))
    tail = local(
        tail_kernel, "tail", sds((chips * CAP, features)), (own, other, own_away, other_away)
    )
    got = over_ctx(tail, masks[-1])
    sums = local(
        functools.partial(total_kernel, groups, chips),
        "total",
        [sds((slots, features))] * (ctx_size - 1),
        (own, other, *parts),
    )
    far_first = sorted(zip(masks, sums), key=lambda pair: -pair[0])
    backs = [over_ctx(p, turn) if turn else p for turn, p in far_first]
    place = {turn: i for i, (turn, _) in enumerate(far_first)}
    order = [place[turn] for turn in masks[:-1]]
    pieces = local(split_kernel, "split", [sds((CAP, features))] * chips, (got,))
    late = [pieces[0]] + [over_chips(pieces[j], j) for j in range(1, chips)]
    return combine(mix, order, groups, backs, late)


def solution(mesh):
    return jax.shard_map(
        shards,
        mesh=mesh,
        in_specs=(
            P(("dp", "ctx"), "tp"),
            P(("dp", "ctx"), None),
            P(("dp", "ctx"), None),
            P(("ctx", "tp"), None, None),
            P(("ctx", "tp"), None, None),
            P(("ctx", "tp"), None, None),
        ),
        out_specs=P(("dp", "ctx"), "tp"),
        check_vma=False,
    )
```
